32 devices in a mesh: dp: 8 (over y, x, core), expert: 4 (over z).
Axes of the slice: x: 2, y: 2, z: 4, core: 2. Of those that a mesh axis runs over, the one named last changes fastest.
Arguments:
- residual: bfloat16 [4096, 2048], P(('dp', 'expert')), may hold values from -6 to 6
- grad_stream: bfloat16 [4096, 2048], P(('dp', 'expert')), may hold values from -6 to 6
- expert_gain: float32 [2048], replicated, may hold values from 0.5 to 1.5
- router_weight: bfloat16 [2048, 32], replicated, may hold values from -0.125 to 0.125
- gate_up_weight: bfloat16 [32, 2048, 1536], P('expert', 'dp'), may hold values from -0.125 to 0.125
- down_weight: bfloat16 [32, 2048, 768], P('expert', 'dp'), may hold values from -0.21875 to 0.21875
- need_lists: int32 [4, 2], replicated, may hold values from 0 to 31, as said below
- routes: int32 [4096, 1], P(('dp', 'expert')), may hold values from 0 to 1
Outputs:
- stream: bfloat16 [4096, 2048], P(('dp', 'expert'))
- grad_residual: bfloat16 [4096, 2048], P(('dp', 'expert'))
The draws below stay inside these ranges and needn't reach their ends.
Inputs may be any that keep to these rules, and one draw needn't show every extreme that they name: `need_lists`: row c lists 2 experts with different owner indices (expert id // 8).
All inputs are finite; a program needn't handle non-finite values.
Results may differ from the reference program's by a relative error of at most 0.008.
Values may be sent and summed in bfloat16 or wider, within the bound.
A program may use at most 128 MiB of HBM per device.

```python
import jax
import jax.numpy as jnp
from jax import lax

D = 2048
FB = 768
EXP_DEV = 8
NEED = 2
TOP = 1
T_DEV = 128
EXPERTS = 32
TOKENS = 4096
N_DP = 8
N_EXPERT = 4


def draw_need_lists(key, part):
    columns = jnp.arange(N_EXPERT, dtype=jnp.int32)
    rotate = jax.random.randint(jax.random.fold_in(key, 11), (), 0, 3)
    offsets = jnp.array([1, N_EXPERT - 1, N_EXPERT // 2], dtype=jnp.int32)
    first = (columns + jnp.take(offsets, (columns + rotate) % 3)) % N_EXPERT
    extra = jax.random.randint(jax.random.fold_in(key, 12), (N_EXPERT,), 0, N_EXPERT - 1)
    second = (first + 1 + extra) % N_EXPERT
    order = jax.random.randint(jax.random.fold_in(key, 13), (N_EXPERT,), 0, 2)
    owner_a = jnp.where(order == 0, first, second)
    owner_b = jnp.where(order == 0, second, first)
    local_ids = jax.random.randint(jax.random.fold_in(key, 14), (N_EXPERT, 2), 0, EXP_DEV)
    lists = jnp.stack([owner_a, owner_b], axis=1) * EXP_DEV + local_ids
    top_id = jnp.array(N_EXPERT * EXP_DEV - 1, dtype=jnp.int32)
    low_id = jnp.array(0, dtype=jnp.int32)
    row_zero = jnp.where(order[0] == 0, jnp.stack([top_id, low_id]), jnp.stack([low_id, top_id]))
    lists = jnp.where((columns == 0)[:, None], row_zero[None, :], lists)
    return lists.astype(jnp.int32)


def block_scale(key, shape, shards, smallest, high):
    factor_of = 1.0
    for position, shards_of in shards:
        draws = jax.random.uniform(jax.random.fold_in(jax.random.fold_in(key, 6), position), (shards_of,), jnp.float32, smallest / len(shards), high / len(shards))
        factor_of = factor_of * jnp.repeat(jnp.exp(draws), shape[position] // shards_of).reshape((-1,) + (1,) * (len(shape) - 1 - position))
    return factor_of


def distinct(key, rows, amount, top, lift):
    sequence = jax.random.permutation(jax.random.fold_in(key, 1), amount)
    favour = sequence
    for power in range(3):
        favour = favour * favour // amount
    favour = favour * lift // amount
    tickets = jax.random.randint(jax.random.fold_in(key, 2), (rows, amount), 0, 4096) + favour
    holders = jax.random.permutation(jax.random.fold_in(key, 3), rows)[jnp.arange(amount) % rows]
    tickets = jnp.where(jnp.arange(rows)[:, None] == holders[None, :], 1 << 14, tickets)
    merit = tickets * amount + jnp.arange(amount)
    return lax.top_k(merit.astype(jnp.int32), top)[1].astype(jnp.int32)


def bell_draw(rng, extent, scale, reach, shards=(), kind=jnp.bfloat16):
    values = jax.random.normal(rng, extent, jnp.float32) * scale
    if len(shards) > 0:
        values = block_scale(rng, extent, shards, -0.22, 0.18) * values
    return jnp.clip(values, min=-reach, max=reach).astype(kind)


def setup_inputs(seed: int = 0) -> dict:
    splits = jax.random.split(jax.random.key(seed), 9)
    return {
        "residual": bell_draw(splits[0], (TOKENS, D), 1.0, 6.0, ((0, 32),)),
        "grad_stream": bell_draw(splits[1], (TOKENS, D), 1.0, 6.0, ((0, 32),)),
        "expert_gain": jnp.clip(1.0 + 0.1 * jax.random.normal(splits[2], (D,), jnp.float32), 0.5, 1.5),
        "router_weight": bell_draw(splits[3], (D, EXPERTS), D ** -0.5, 0.125),
        "gate_up_weight": bell_draw(splits[4], (EXPERTS, D, 2 * FB), D ** -0.5, 0.125, ((0, 4), (1, 8))),
        "down_weight": bell_draw(splits[5], (EXPERTS, D, FB), FB ** -0.5, 0.21875, ((0, 4), (1, 8))),
        "need_lists": draw_need_lists(jax.random.fold_in(splits[8], 71), 0),
        "routes": distinct(splits[7], TOKENS, NEED, TOP, 4096),
    }


eps = 1e-05

def norm_factor(values):
    return lax.rsqrt(lax.optimization_barrier(jnp.mean(values * values, axis=-1, keepdims=True)) + eps)

def norm_backward(values, factor, gain, grad):
    scaled = gain * grad
    return factor * scaled - values * factor ** 3 * lax.optimization_barrier(jnp.mean(values * scaled, axis=-1, keepdims=True))

def ein(spec, left, right):
    return jnp.einsum(spec, left.astype(jnp.float32), right.astype(jnp.float32))

def local_block(residual, grad_stream, expert_gain, router_cols, gate_up, down, routes):
    width = down.shape[2]
    stream_in = residual.astype(jnp.float32)
    factor_in = norm_factor(stream_in)
    normed = (stream_in * factor_in * expert_gain).astype(jnp.bfloat16)
    logits = jnp.dot(normed, router_cols, preferred_element_type=jnp.float32)
    gates = jax.nn.sigmoid(logits - logits[:, ::-1])
    select = (routes[:, 0:1] == jnp.arange(2, dtype=jnp.int32)[None, :]).astype(jnp.float32)
    mix = gates * select
    hidden = ein('td,ndf->ntf', normed, gate_up)
    gate_part = hidden[:, :, :width]
    up_part = hidden[:, :, width:]
    sigma = jax.nn.sigmoid(gate_part)
    silu_gate = gate_part * sigma
    act = (silu_gate * up_part).astype(jnp.bfloat16)
    branch = ein('ntf,ndf->ntd', act, down).astype(jnp.bfloat16)
    branch_f = branch.astype(jnp.float32)
    stream = (stream_in + jnp.einsum('tn,ntd->td', mix, branch_f)).astype(jnp.bfloat16)
    grad_out = grad_stream.astype(jnp.float32)
    grad_mix = jnp.einsum('ntd,td->tn', branch_f, grad_out)
    grad_branch = (jnp.transpose(mix)[:, :, None] * grad_out[None]).astype(jnp.bfloat16)
    grad_act = ein('ntd,ndf->ntf', grad_branch, down)
    slope = sigma * (1.0 + gate_part * (1.0 - sigma))
    grad_hidden = jnp.concatenate([grad_act * up_part * slope, grad_act * silu_gate], axis=-1).astype(jnp.bfloat16)
    expert_term = ein('ntf,ndf->ntd', grad_hidden, gate_up).astype(jnp.bfloat16)
    grad_gates = grad_mix * select
    grad_logits = (gates * (grad_gates - lax.optimization_barrier(jnp.sum(gates * grad_gates, axis=-1, keepdims=True)))).astype(jnp.bfloat16)
    grad_normed = lax.optimization_barrier(jnp.sum(expert_term.astype(jnp.float32), axis=0)) + ein('tn,dn->td', grad_logits, router_cols)
    grad_residual = (grad_out + norm_backward(stream_in, factor_in, expert_gain, grad_normed)).astype(jnp.bfloat16)
    return (stream, grad_residual)

def reference(residual, grad_stream, expert_gain, router_weight, gate_up_weight, down_weight, need_lists, routes):
    blocks_in = residual.reshape(N_DP, N_EXPERT, T_DEV, D)
    blocks_grad = grad_stream.reshape(N_DP, N_EXPERT, T_DEV, D)
    blocks_route = routes.reshape(N_DP, N_EXPERT, T_DEV, TOP)

    def column(carry, col):
        listed = need_lists[col]
        router_cols = jnp.take(router_weight, listed, axis=1)
        gate_up = jnp.take(gate_up_weight, listed, axis=0)
        down = jnp.take(down_weight, listed, axis=0)
        res_col = lax.dynamic_index_in_dim(blocks_in, col, 1, keepdims=False).reshape(N_DP * T_DEV, D)
        grad_col = lax.dynamic_index_in_dim(blocks_grad, col, 1, keepdims=False).reshape(N_DP * T_DEV, D)
        route_col = lax.dynamic_index_in_dim(blocks_route, col, 1, keepdims=False).reshape(N_DP * T_DEV, TOP)
        stream, grad_res = local_block(res_col, grad_col, expert_gain, router_cols, gate_up, down, route_col)
        return (carry, (stream, grad_res))
    carry, (streams, grads) = lax.scan(column, jnp.zeros((), jnp.float32), jnp.arange(N_EXPERT, dtype=jnp.int32))
    stream = jnp.transpose(streams.reshape(N_EXPERT, N_DP, T_DEV, D), (1, 0, 2, 3)).reshape(TOKENS, D)
    grad_residual = jnp.transpose(grads.reshape(N_EXPERT, N_DP, T_DEV, D), (1, 0, 2, 3)).reshape(TOKENS, D)
    return (stream, grad_residual)
```

```python
import functools

import jax
import jax.numpy as jnp
from jax import lax
from jax.experimental import pallas as pl
from jax.experimental.pallas import tpu as pltpu
from jax.sharding import PartitionSpec as P

eps = 1e-05
MESH = pl.DeviceIdType.MESH


def partner(value, axis, stride):
    mask = 2**stride
    pairs = [(source, source ^ mask) for source in range(lax.axis_size(axis))]
    return lax.ppermute(value, axis, pairs)


def norm_factor(values):
    return lax.rsqrt(jnp.mean(values * values, axis=-1, keepdims=True) + eps)


def norm_backward(values, factor, gain, grad):
    scaled = gain * grad
    return factor * scaled - values * factor**3 * jnp.mean(values * scaled, axis=-1, keepdims=True)


def pick_kernel(columns, slots, need_ref, gate_up_ref, down_ref, out_ref, sems):
    column = lax.axis_index("expert")
    held = gate_up_ref.shape[0]
    joined = gate_up_ref.shape[2]
    width = down_ref.shape[2]
    copies = []
    for j in range(columns):
        pick = jnp.int32(0)
        for s in range(slots):
            expert = need_ref[j, s]
            pick = jnp.where(expert // held == column, expert % held, pick)
        copies.append(
            pltpu.make_async_copy(
                gate_up_ref.at[pick], out_ref.at[j, :, pl.ds(0, joined)], sems.at[j, 0]
            )
        )
        copies.append(
            pltpu.make_async_copy(
                down_ref.at[pick], out_ref.at[j, :, pl.ds(joined, width)], sems.at[j, 1]
            )
        )
    for copy in copies:
        copy.start()
    for copy in copies:
        copy.wait()


def pick(need_lists, gate_up_weight, down_weight):
    columns, slots = need_lists.shape
    rows = down_weight.shape[1]
    total = gate_up_weight.shape[2] + down_weight.shape[2]
    return pl.pallas_call(
        functools.partial(pick_kernel, columns, slots),
        out_shape=jax.ShapeDtypeStruct((columns, rows, total), jnp.bfloat16),
        in_specs=[
            pl.BlockSpec(memory_space=pltpu.SMEM),
            pl.BlockSpec(memory_space=pl.ANY),
            pl.BlockSpec(memory_space=pl.ANY),
        ],
        out_specs=pl.BlockSpec(memory_space=pl.ANY),
        scratch_shapes=[pltpu.SemaphoreType.DMA((columns, 2))],
    )(need_lists, gate_up_weight, down_weight)


def move_kernel(columns, ranks, held, chunks, need_ref, out_ref, weights_ref, *scratch):
    arrived = scratch[:chunks]
    slots = scratch[chunks : 2 * chunks]
    zs, zr, ps, pr, own = scratch[2 * chunks :]
    column = lax.axis_index("expert")
    me = lax.axis_index("dp")
    rows = out_ref.shape[1]
    part = rows // chunks
    depth = 2

    barrier = pltpu.get_barrier_semaphore()
    for k in range(1, columns):
        pl.semaphore_signal(
            barrier, inc=1, device_id=(me, lax.rem(column + k, columns)), device_id_type=MESH
        )
    for k in range(1, ranks):
        pl.semaphore_signal(
            barrier, inc=1, device_id=(lax.rem(me + k, ranks), column), device_id_type=MESH
        )
    pl.semaphore_wait(barrier, columns + ranks - 2)

    def own_copy(c):
        return pltpu.make_async_copy(
            out_ref.at[column, pl.ds(c * part, part)], arrived[c].at[column], own.at[c]
        )

    def column_copy(c, k):
        to = lax.rem(column + k, columns)
        return pltpu.make_async_remote_copy(
            src_ref=out_ref.at[to, pl.ds(c * part, part)],
            dst_ref=arrived[c].at[column],
            send_sem=zs.at[k - 1, c],
            recv_sem=zr.at[k - 1, c],
            device_id=(me, to),
            device_id_type=MESH,
        )

    place = pl.multiple_of(me * rows, rows)

    def spread_copy(c, k):
        to = lax.rem(me + k, ranks)
        return pltpu.make_async_remote_copy(
            src_ref=slots[c].at[lax.rem(to, 2)],
            dst_ref=weights_ref.at[pl.ds(place + c * part, part)],
            send_sem=ps.at[k - 1, c],
            recv_sem=pr.at[k - 1, c],
            device_id=(to, column),
            device_id_type=MESH,
        )

    def keep_copy(c):
        return pltpu.make_async_copy(
            slots[c].at[lax.rem(me, 2)],
            weights_ref.at[pl.ds(place + c * part, part)],
            own.at[chunks + c],
        )

    def start_columns(c):
        own_copy(c).start()
        for k in range(1, columns):
            column_copy(c, k).start()

    for c in range(min(depth, chunks)):
        start_columns(c)
    for c in range(chunks):
        own_copy(c).wait()
        for k in range(1, columns):
            column_copy(c, k).wait_recv()
        if c + depth < chunks:
            for k in range(1, columns):
                column_copy(c, k).wait_send()
            start_columns(c + depth)
        for s in range(2):
            owner = need_ref[column, s] // held
            slots[c][s] = arrived[c][owner]
        for k in range(1, ranks):
            spread_copy(c, k).start()
        keep_copy(c).start()
    for c in range(max(chunks - depth, 0), chunks):
        for k in range(1, columns):
            column_copy(c, k).wait_send()
    for c in range(chunks):
        keep_copy(c).wait()
        for k in range(1, ranks):
            spread_copy(c, k).wait()


def move(need_lists, outgoing, held, ranks):
    columns, rows, total = outgoing.shape
    chunks = max(1, min(8, rows // 32))
    part = rows // chunks
    return pl.pallas_call(
        functools.partial(move_kernel, columns, ranks, held, chunks),
        out_shape=jax.ShapeDtypeStruct((ranks * rows, total), jnp.bfloat16),
        in_specs=[
            pl.BlockSpec(memory_space=pltpu.SMEM),
            pl.BlockSpec(memory_space=pl.ANY),
        ],
        out_specs=pl.BlockSpec(memory_space=pl.ANY),
        scratch_shapes=[pltpu.VMEM((columns, part, total), jnp.bfloat16) for _ in range(chunks)]
        + [pltpu.VMEM((2, part, total), jnp.bfloat16) for _ in range(chunks)]
        + [
            pltpu.SemaphoreType.DMA((columns - 1, chunks)),
            pltpu.SemaphoreType.DMA((columns - 1, chunks)),
            pltpu.SemaphoreType.DMA((ranks - 1, chunks)),
            pltpu.SemaphoreType.DMA((ranks - 1, chunks)),
            pltpu.SemaphoreType.DMA((2 * chunks,)),
        ],
        compiler_params=pltpu.CompilerParams(
            collective_id=0, has_side_effects=True, vmem_limit_bytes=40 * 1024 * 1024
        ),
    )(need_lists, outgoing)


def body(
    residual,
    grad_stream,
    expert_gain,
    router_weight,
    gate_up_weight,
    down_weight,
    need_lists,
    routes,
):
    column = lax.axis_index("expert")
    ranks = lax.axis_size("dp")
    parity = lax.axis_index("dp") % 2
    held = gate_up_weight.shape[0]
    width = down_weight.shape[2]
    tokens = residual.shape[0]
    listed = lax.dynamic_index_in_dim(need_lists, column, 0, keepdims=False)
    outgoing = pick(need_lists, gate_up_weight, down_weight)
    stream_in = residual.astype(jnp.float32)
    factor_in = norm_factor(stream_in)
    normed = (stream_in * factor_in * expert_gain).astype(jnp.bfloat16)
    router_cols = jnp.take(router_weight, listed, axis=1)
    logits = jnp.dot(normed, router_cols, preferred_element_type=jnp.float32)
    gates = jax.nn.sigmoid(logits - logits[:, ::-1])
    select = (routes == jnp.arange(2, dtype=jnp.int32)[None, :]).astype(jnp.float32)
    mix = gates * select
    mix_here = lax.dynamic_index_in_dim(mix, parity, 1, keepdims=False)
    mix_there = lax.dynamic_index_in_dim(mix, 1 - parity, 1, keepdims=False)
    grad_out = grad_stream.astype(jnp.float32)
    send_grad = (mix_there[:, None] * grad_out).astype(jnp.bfloat16)
    partner_normed, partner_grad = partner((normed, send_grad), "dp", 0)
    pair_normed = jnp.concatenate([normed, partner_normed], axis=0)
    weights = move(need_lists, outgoing, held, ranks)
    gate_up = weights[:, : 2 * width]
    down = weights[:, 2 * width :]
    hidden = jnp.dot(pair_normed, gate_up, preferred_element_type=jnp.float32)
    gate_part = hidden[:, :width]
    up_part = hidden[:, width:]
    sigma = jax.nn.sigmoid(gate_part)
    silu_gate = gate_part * sigma
    act = (silu_gate * up_part).astype(jnp.bfloat16)
    branch = jnp.einsum("tf,df->td", act, down, preferred_element_type=jnp.float32).astype(
        jnp.bfloat16
    )
    other_branch = partner(branch[tokens:], "dp", 0)
    branch_here = branch[:tokens].astype(jnp.float32)
    branch_there = other_branch.astype(jnp.float32)
    stream = (
        stream_in + mix_here[:, None] * branch_here + mix_there[:, None] * branch_there
    ).astype(jnp.bfloat16)
    mix_grad_here = jnp.sum(branch_here * grad_out, axis=-1)
    mix_grad_there = jnp.sum(branch_there * grad_out, axis=-1)
    grad_mix = jnp.where(
        parity == 0,
        jnp.stack([mix_grad_here, mix_grad_there], axis=1),
        jnp.stack([mix_grad_there, mix_grad_here], axis=1),
    )
    grad_branch = jnp.concatenate(
        [(mix_here[:, None] * grad_out).astype(jnp.bfloat16), partner_grad], axis=0
    )
    grad_act = jnp.einsum("td,df->tf", grad_branch, down, preferred_element_type=jnp.float32)
    slope = sigma * (1.0 + gate_part * (1.0 - sigma))
    grad_hidden = jnp.concatenate(
        [grad_act * up_part * slope, grad_act * silu_gate], axis=1
    ).astype(jnp.bfloat16)
    expert_term = jnp.einsum(
        "tk,dk->td", grad_hidden, gate_up, preferred_element_type=jnp.float32
    ).astype(jnp.bfloat16)
    other_term = partner(expert_term[tokens:], "dp", 0)
    grad_gates = grad_mix * select
    grad_logits = (
        gates * (grad_gates - jnp.sum(gates * grad_gates, axis=-1, keepdims=True))
    ).astype(jnp.bfloat16)
    grad_normed = expert_term[:tokens].astype(jnp.float32) + other_term.astype(jnp.float32)
    grad_normed = grad_normed + jnp.einsum(
        "tn,dn->td", grad_logits, router_cols, preferred_element_type=jnp.float32
    )
    grad_residual = (
        grad_out + norm_backward(stream_in, factor_in, expert_gain, grad_normed)
    ).astype(jnp.bfloat16)
    return (stream, grad_residual)


def solution(mesh):
    return jax.shard_map(
        body,
        mesh=mesh,
        in_specs=(
            P(("dp", "expert"), None),
            P(("dp", "expert"), None),
            P(),
            P(),
            P("expert", "dp", None),
            P("expert", "dp", None),
            P(),
            P(("dp", "expert"), None),
        ),
        out_specs=(P(("dp", "expert"), None), P(("dp", "expert"), None)),
        check_vma=False,
    )
```

```python
import functools

import jax
import jax.numpy as jnp
from jax import lax
from jax.experimental import pallas as pl
from jax.experimental.pallas import tpu as pltpu
from jax.sharding import PartitionSpec as P

eps = 1e-05
MESH = pl.DeviceIdType.MESH


def norm_factor(values):
    return lax.rsqrt(jnp.mean(values * values, axis=-1, keepdims=True) + eps)


def norm_backward(values, factor, gain, grad):
    scaled = gain * grad
    return factor * scaled - values * factor**3 * jnp.mean(values * scaled, axis=-1, keepdims=True)


def block_kernel(
    columns,
    ranks,
    need_ref,
    gate_up_ref,
    down_ref,
    normed_ref,
    grad_here_ref,
    grad_there_ref,
    branch_here,
    branch_there,
    term_here,
    term_there,
    *scratch,
):
    held, rows, _ = down_ref.shape
    width = down_ref.shape[2]
    slice_ = 128
    parts = width // slice_
    tokens = normed_ref.shape[0]
    local = scratch[:parts]
    arrived = scratch[parts : 2 * parts]
    (src, stage, weights, pair_x, pair_g, sum_b, sum_t, back_b, back_t) = scratch[
        2 * parts : 2 * parts + 9
    ]
    ld, zs, zr, ps, pr, ts, tr = scratch[2 * parts + 9 :]
    column = lax.axis_index("expert")
    me = lax.axis_index("dp")
    core = lax.rem(me, 2)
    sibling = me + 1 - 2 * core
    square = ranks == 8
    depth = 2

    def loads(c):
        return [
            pltpu.make_async_copy(
                ref.at[:, :, pl.ds(start, slice_)],
                local[c].at[:, :, pl.ds(i * slice_, slice_)],
                ld.at[c, i],
            )
            for i, (ref, start) in enumerate(
                (
                    (gate_up_ref, c * slice_),
                    (gate_up_ref, width + c * slice_),
                    (down_ref, c * slice_),
                )
            )
        ]

    for c in range(parts):
        for copy in loads(c):
            copy.start()

    if square:
        beside = me + 2 - 4 * lax.rem(me // 2, 2)
        across = me + 4 - 8 * (me // 4)
        peers = [sibling, beside, across]
    else:
        peers = [lax.rem(me + k, ranks) for k in range(1, ranks)]
    barrier = pltpu.get_barrier_semaphore()
    for k in range(1, columns):
        pl.semaphore_signal(
            barrier, inc=1, device_id=(me, lax.rem(column + k, columns)), device_id_type=MESH
        )
    for peer in peers:
        pl.semaphore_signal(barrier, inc=1, device_id=(peer, column), device_id_type=MESH)
    pl.semaphore_wait(barrier, columns - 1 + len(peers))

    def to_sibling(i, source, target):
        return pltpu.make_async_remote_copy(
            src_ref=source,
            dst_ref=target,
            send_sem=ts.at[i],
            recv_sem=tr.at[i],
            device_id=(sibling, column),
            device_id_type=MESH,
        )

    def token_copies():
        return [
            to_sibling(0, normed_ref, pair_x.at[pl.ds(tokens, tokens)]),
            to_sibling(1, grad_there_ref, pair_g.at[pl.ds(tokens, tokens)]),
        ]

    for copy in token_copies():
        copy.start()

    def column_copy(c, k):
        return pltpu.make_async_remote_copy(
            src_ref=src.at[c, k - 1],
            dst_ref=arrived[c].at[column],
            send_sem=zs.at[k - 1, c],
            recv_sem=zr.at[k - 1, c],
            device_id=(me, lax.rem(column + k, columns)),
            device_id_type=MESH,
        )

    def pick(to):
        found = jnp.int32(0)
        for s in range(2):
            expert = need_ref[to, s]
            found = jnp.where(expert // held == column, expert % held, found)
        return found

    picks = [pick(lax.rem(column + k, columns)) for k in range(columns)]
    owner_mine = need_ref[column, core] // held
    owner_other = need_ref[column, 1 - core] // held

    def start_columns(c):
        for copy in loads(c):
            copy.wait()
        for k in range(1, columns):
            src[c, k - 1] = local[c][picks[k]]
            column_copy(c, k).start()
        arrived[c][column] = local[c][picks[0]]

    def block(c, rank):
        return weights.at[c, pl.ds(pl.multiple_of(rank * rows, rows), rows)]

    def spread(c, i, source, rank, to):
        return pltpu.make_async_remote_copy(
            src_ref=source,
            dst_ref=block(c, rank),
            send_sem=ps.at[i, c],
            recv_sem=pr.at[i, c],
            device_id=(to, column),
            device_id_type=MESH,
        )

    if square:
        beside_rank = beside
        across_other = across + 1 - 2 * core

        def spreads(c):
            mine, other = block(c, me), stage.at[c]
            return [
                spread(c, 0, other, me, sibling),
                spread(c, 1, mine, me, beside),
                spread(c, 2, mine, me, across),
                spread(c, 3, block(c, sibling), sibling, beside),
                spread(c, 4, block(c, sibling), sibling, across),
                spread(c, 5, block(c, beside_rank), beside_rank, across),
                spread(c, 6, block(c, across_other), across_other, beside),
            ]

        def first(c):
            copies = spreads(c)
            for i in (0, 1, 2):
                copies[i].start()

        def second(c):
            copies = spreads(c)
            copies[0].wait_recv()
            copies[3].start()
            copies[4].start()

        def third(c):
            copies = spreads(c)
            copies[1].wait_recv()
            copies[5].start()
            copies[4].wait_recv()
            copies[6].start()

        def last(c):
            copies = spreads(c)
            for i in (2, 3, 5, 6):
                copies[i].wait_recv()
    else:

        def spreads(c):
            return [
                spread(
                    c,
                    k - 1,
                    block(c, me) if k % 2 == 0 else stage.at[c],
                    me,
                    lax.rem(me + k, ranks),
                )
                for k in range(1, ranks)
            ]

        def first(c):
            for copy in spreads(c):
                copy.start()

        def second(c):
            pass

        def third(c):
            pass

        def last(c):
            for copy in spreads(c):
                copy.wait_recv()

    def dot(left, right):
        return jnp.dot(left, right, preferred_element_type=jnp.float32)

    def dot_t(left, right):
        return lax.dot_general(
            left, right, (((1,), (1,)), ((), ())), preferred_element_type=jnp.float32
        )

    def work(c):
        hidden = dot(pair_x[...], weights[c, :, : 2 * slice_])
        grad_act = dot(pair_g[...], weights[c, :, 2 * slice_ :])
        gate_part = hidden[:, :slice_]
        up_part = hidden[:, slice_:]
        sigma = jax.nn.sigmoid(gate_part)
        silu_gate = gate_part * sigma
        act = (silu_gate * up_part).astype(jnp.bfloat16)
        slope = sigma * (1.0 + gate_part * (1.0 - sigma))
        grad_hidden = jnp.concatenate(
            [grad_act * up_part * slope, grad_act * silu_gate], axis=1
        ).astype(jnp.bfloat16)
        branch = dot_t(act, weights[c, :, 2 * slice_ :])
        term = dot_t(grad_hidden, weights[c, :, : 2 * slice_])
        if c == 0:
            sum_b[...] = branch
            sum_t[...] = term
        else:
            sum_b[...] += branch
            sum_t[...] += term

    for c in range(min(depth, parts)):
        start_columns(c)
    pair_x[pl.ds(0, tokens)] = normed_ref[...]
    pair_g[pl.ds(0, tokens)] = grad_here_ref[...]
    for c in range(parts + 2):
        if c < parts:
            for k in range(1, columns):
                column_copy(c, k).wait_recv()
            weights[c, pl.ds(pl.multiple_of(me * rows, rows), rows)] = arrived[c][owner_mine]
            stage[c] = arrived[c][owner_other]
            first(c)
            if c + depth < parts:
                start_columns(c + depth)
            second(c)
        if 1 <= c <= parts:
            third(c - 1)
        if c >= 2:
            last(c - 2)
            if c == 2:
                for copy in token_copies():
                    copy.wait()
            work(c - 2)

    back_b[...] = sum_b[pl.ds(tokens, tokens)].astype(jnp.bfloat16)
    back_t[...] = sum_t[pl.ds(tokens, tokens)].astype(jnp.bfloat16)
    backs = [to_sibling(2, back_b, branch_there), to_sibling(3, back_t, term_there)]
    for copy in backs:
        copy.start()
    branch_here[...] = sum_b[pl.ds(0, tokens)].astype(jnp.bfloat16)
    term_here[...] = sum_t[pl.ds(0, tokens)].astype(jnp.bfloat16)
    for c in range(parts):
        for k in range(1, columns):
            column_copy(c, k).wait_send()
        for copy in spreads(c):
            copy.wait_send()
    for copy in backs:
        copy.wait()


def experts(need_lists, gate_up_weight, down_weight, normed, grad_here, grad_there, ranks):
    columns = need_lists.shape[0]
    held, rows, width = down_weight.shape
    tokens, model = normed.shape
    slice_ = 128
    parts = width // slice_
    vmem = pl.BlockSpec(memory_space=pltpu.VMEM)
    any_ = pl.BlockSpec(memory_space=pl.ANY)
    sent = 7 if ranks == 8 else ranks - 1
    bf16, f32 = jnp.bfloat16, jnp.float32
    return pl.pallas_call(
        functools.partial(block_kernel, columns, ranks),
        out_shape=[jax.ShapeDtypeStruct((tokens, model), bf16)] * 4,
        in_specs=[pl.BlockSpec(memory_space=pltpu.SMEM), any_, any_, vmem, vmem, vmem],
        out_specs=[vmem] * 4,
        scratch_shapes=[pltpu.VMEM((held, rows, 3 * slice_), bf16) for _ in range(parts)]
        + [pltpu.VMEM((columns, rows, 3 * slice_), bf16) for _ in range(parts)]
        + [
            pltpu.VMEM((parts, columns - 1, rows, 3 * slice_), bf16),
            pltpu.VMEM((parts, rows, 3 * slice_), bf16),
            pltpu.VMEM((parts, ranks * rows, 3 * slice_), bf16),
            pltpu.VMEM((2 * tokens, model), bf16),
            pltpu.VMEM((2 * tokens, model), bf16),
            pltpu.VMEM((2 * tokens, model), f32),
            pltpu.VMEM((2 * tokens, model), f32),
            pltpu.VMEM((tokens, model), bf16),
            pltpu.VMEM((tokens, model), bf16),
            pltpu.SemaphoreType.DMA((parts, 3)),
            pltpu.SemaphoreType.DMA((columns - 1, parts)),
            pltpu.SemaphoreType.DMA((columns - 1, parts)),
            pltpu.SemaphoreType.DMA((sent, parts)),
            pltpu.SemaphoreType.DMA((sent, parts)),
            pltpu.SemaphoreType.DMA((4,)),
            pltpu.SemaphoreType.DMA((4,)),
        ],
        compiler_params=pltpu.CompilerParams(
            collective_id=0, has_side_effects=True, vmem_limit_bytes=56 * 1024 * 1024
        ),
    )(need_lists, gate_up_weight, down_weight, normed, grad_here, grad_there)


def body(
    residual,
    grad_stream,
    expert_gain,
    router_weight,
    gate_up_weight,
    down_weight,
    need_lists,
    routes,
):
    column = lax.axis_index("expert")
    ranks = lax.axis_size("dp")
    parity = lax.axis_index("dp") % 2
    listed = lax.dynamic_index_in_dim(need_lists, column, 0, keepdims=False)
    stream_in = residual.astype(jnp.float32)
    factor_in = norm_factor(stream_in)
    normed = (stream_in * factor_in * expert_gain).astype(jnp.bfloat16)
    router_cols = jnp.take(router_weight, listed, axis=1)
    logits = jnp.dot(normed, router_cols, preferred_element_type=jnp.float32)
    gates = jax.nn.sigmoid(logits - logits[:, ::-1])
    select = (routes == jnp.arange(2, dtype=jnp.int32)[None, :]).astype(jnp.float32)
    mix = gates * select
    mix_here = lax.dynamic_index_in_dim(mix, parity, 1, keepdims=False)
    mix_there = lax.dynamic_index_in_dim(mix, 1 - parity, 1, keepdims=False)
    grad_out = grad_stream.astype(jnp.float32)
    grad_here = (mix_here[:, None] * grad_out).astype(jnp.bfloat16)
    grad_there = (mix_there[:, None] * grad_out).astype(jnp.bfloat16)
    branch_here, branch_there, term_here, term_there = experts(
        need_lists, gate_up_weight, down_weight, normed, grad_here, grad_there, ranks
    )
    branch_here = branch_here.astype(jnp.float32)
    branch_there = branch_there.astype(jnp.float32)
    stream = (
        stream_in + mix_here[:, None] * branch_here + mix_there[:, None] * branch_there
    ).astype(jnp.bfloat16)
    mix_grad_here = jnp.sum(branch_here * grad_out, axis=-1)
    mix_grad_there = jnp.sum(branch_there * grad_out, axis=-1)
    grad_mix = jnp.where(
        parity == 0,
        jnp.stack([mix_grad_here, mix_grad_there], axis=1),
        jnp.stack([mix_grad_there, mix_grad_here], axis=1),
    )
    grad_gates = grad_mix * select
    grad_logits = (
        gates * (grad_gates - jnp.sum(gates * grad_gates, axis=-1, keepdims=True))
    ).astype(jnp.bfloat16)
    grad_normed = term_here.astype(jnp.float32) + term_there.astype(jnp.float32)
    grad_normed = grad_normed + jnp.einsum(
        "tn,dn->td", grad_logits, router_cols, preferred_element_type=jnp.float32
    )
    grad_residual = (
        grad_out + norm_backward(stream_in, factor_in, expert_gain, grad_normed)
    ).astype(jnp.bfloat16)
    return (stream, grad_residual)


def solution(mesh):
    return jax.shard_map(
        body,
        mesh=mesh,
        in_specs=(
            P(("dp", "expert"), None),
            P(("dp", "expert"), None),
            P(),
            P(),
            P("expert", "dp", None),
            P("expert", "dp", None),
            P(),
            P(("dp", "expert"), None),
        ),
        out_specs=(P(("dp", "expert"), None), P(("dp", "expert"), None)),
        check_vma=False,
    )
```

```python
import functools

import jax
import jax.numpy as jnp
from jax import lax
from jax.experimental import pallas as pl
from jax.experimental.pallas import tpu as pltpu
from jax.sharding import PartitionSpec as P

eps = 1e-05
MESH = pl.DeviceIdType.MESH


def norm_factor(values):
    return lax.rsqrt(jnp.mean(values * values, axis=-1, keepdims=True) + eps)


def norm_backward(values, factor, gain, grad):
    scaled = gain * grad
    return factor * scaled - values * factor**3 * jnp.mean(values * scaled, axis=-1, keepdims=True)


def block_kernel(
    columns,
    ranks,
    relays,
    need_ref,
    gate_up_ref,
    down_ref,
    normed_ref,
    grad_here_ref,
    grad_there_ref,
    branch_here,
    branch_there,
    term_here,
    term_there,
    *scratch,
):
    held, rows, _ = down_ref.shape
    width = down_ref.shape[2]
    slice_ = 128
    parts = width // slice_
    tokens = normed_ref.shape[0]
    local = scratch[:parts]
    arrived = scratch[parts : 2 * parts]
    (src, stage, weights, pair_x, pair_g, sum_b, sum_t, back_b, back_t) = scratch[
        2 * parts : 2 * parts + 9
    ]
    ld, zs, zr, ps, pr, ts, tr = scratch[2 * parts + 9 :]
    column = lax.axis_index("expert")
    me = lax.axis_index("dp")
    core = lax.rem(me, 2)
    sibling = me + 1 - 2 * core
    square = ranks == 8
    depth = 2

    def loads(c):
        return [
            pltpu.make_async_copy(
                ref.at[:, :, pl.ds(start, slice_)],
                local[c].at[:, :, pl.ds(i * slice_, slice_)],
                ld.at[c, i],
            )
            for i, (ref, start) in enumerate(
                (
                    (gate_up_ref, c * slice_),
                    (gate_up_ref, width + c * slice_),
                    (down_ref, c * slice_),
                )
            )
        ]

    for c in range(parts):
        for copy in loads(c):
            copy.start()

    if square:
        beside = me + 2 - 4 * lax.rem(me // 2, 2)
        across = me + 4 - 8 * (me // 4)
        peers = [sibling, beside, across]
    else:
        peers = [lax.rem(me + k, ranks) for k in range(1, ranks)]
    barrier = pltpu.get_barrier_semaphore()
    for k in range(1, columns):
        pl.semaphore_signal(
            barrier, inc=1, device_id=(me, lax.rem(column + k, columns)), device_id_type=MESH
        )
    for peer in peers:
        pl.semaphore_signal(barrier, inc=1, device_id=(peer, column), device_id_type=MESH)
    pl.semaphore_wait(barrier, columns - 1 + len(peers))

    def to_sibling(i, source, target):
        return pltpu.make_async_remote_copy(
            src_ref=source,
            dst_ref=target,
            send_sem=ts.at[i],
            recv_sem=tr.at[i],
            device_id=(sibling, column),
            device_id_type=MESH,
        )

    def token_copies():
        return [
            to_sibling(0, normed_ref, pair_x.at[pl.ds(tokens, tokens)]),
            to_sibling(1, grad_there_ref, pair_g.at[pl.ds(tokens, tokens)]),
        ]

    for copy in token_copies():
        copy.start()

    def column_copy(c, k):
        return pltpu.make_async_remote_copy(
            src_ref=src.at[c, k - 1],
            dst_ref=arrived[c].at[column],
            send_sem=zs.at[k - 1, c],
            recv_sem=zr.at[k - 1, c],
            device_id=(me, lax.rem(column + k, columns)),
            device_id_type=MESH,
        )

    def pick(to, found):
        for s in range(2):
            expert = need_ref[to, s]
            found = jnp.where(expert // held == column, expert % held, found)
        return found

    picks = []
    for k in range(columns):
        to = lax.rem(column + k, columns)
        found = jnp.int32(0)
        for owner, via, end in relays:
            if (via - owner) % columns == k:
                found = jnp.where(column == owner, pick(end, found), found)
        picks.append(pick(to, found))

    def sends(k):
        yes = column >= 0
        for owner, via, end in relays:
            if (end - owner) % columns == k:
                yes = yes & (column != owner)
        return yes

    def relay_copy(c, i):
        owner, via, end = relays[i]
        return pltpu.make_async_remote_copy(
            src_ref=arrived[c].at[owner],
            dst_ref=arrived[c].at[owner],
            send_sem=zs.at[columns - 1, c],
            recv_sem=zr.at[(end - owner) % columns - 1, c],
            device_id=(me, end),
            device_id_type=MESH,
        )

    def relay(c, act):
        for i, (owner, via, end) in enumerate(relays):

            @pl.when(column == via)
            def _():
                act(relay_copy(c, i))

    owner_mine = need_ref[column, core] // held
    owner_other = need_ref[column, 1 - core] // held

    def start_columns(c):
        for copy in loads(c):
            copy.wait()
        for k in range(1, columns):
            src[c, k - 1] = local[c][picks[k]]

            @pl.when(sends(k))
            def _():
                column_copy(c, k).start()

        arrived[c][column] = local[c][picks[0]]

    def block(c, rank):
        return weights.at[c, pl.ds(pl.multiple_of(rank * rows, rows), rows)]

    def spread(c, i, source, rank, to):
        return pltpu.make_async_remote_copy(
            src_ref=source,
            dst_ref=block(c, rank),
            send_sem=ps.at[i, c],
            recv_sem=pr.at[i, c],
            device_id=(to, column),
            device_id_type=MESH,
        )

    if square:
        beside_rank = beside
        across_other = across + 1 - 2 * core

        def spreads(c):
            mine, other = block(c, me), stage.at[c]
            return [
                spread(c, 0, other, me, sibling),
                spread(c, 1, mine, me, beside),
                spread(c, 2, mine, me, across),
                spread(c, 3, block(c, sibling), sibling, beside),
                spread(c, 4, block(c, sibling), sibling, across),
                spread(c, 5, block(c, beside_rank), beside_rank, across),
                spread(c, 6, block(c, across_other), across_other, beside),
            ]

        def first(c):
            copies = spreads(c)
            for i in (0, 1, 2):
                copies[i].start()

        def second(c):
            copies = spreads(c)
            copies[0].wait_recv()
            copies[3].start()
            copies[4].start()

        def third(c):
            copies = spreads(c)
            copies[1].wait_recv()
            copies[5].start()
            copies[4].wait_recv()
            copies[6].start()

        def last(c):
            copies = spreads(c)
            for i in (2, 3, 5, 6):
                copies[i].wait_recv()
    else:

        def spreads(c):
            return [
                spread(
                    c,
                    k - 1,
                    block(c, me) if k % 2 == 0 else stage.at[c],
                    me,
                    lax.rem(me + k, ranks),
                )
                for k in range(1, ranks)
            ]

        def first(c):
            for copy in spreads(c):
                copy.start()

        def second(c):
            pass

        def third(c):
            pass

        def last(c):
            for copy in spreads(c):
                copy.wait_recv()

    def dot(left, right):
        return jnp.dot(left, right, preferred_element_type=jnp.float32)

    def dot_t(left, right):
        return lax.dot_general(
            left, right, (((1,), (1,)), ((), ())), preferred_element_type=jnp.float32
        )

    def work(c):
        hidden = dot(pair_x[...], weights[c, :, : 2 * slice_])
        grad_act = dot(pair_g[...], weights[c, :, 2 * slice_ :])
        gate_part = hidden[:, :slice_]
        up_part = hidden[:, slice_:]
        sigma = jax.nn.sigmoid(gate_part)
        silu_gate = gate_part * sigma
        act = (silu_gate * up_part).astype(jnp.bfloat16)
        slope = sigma * (1.0 + gate_part * (1.0 - sigma))
        grad_hidden = jnp.concatenate(
            [grad_act * up_part * slope, grad_act * silu_gate], axis=1
        ).astype(jnp.bfloat16)
        branch = dot_t(act, weights[c, :, 2 * slice_ :])
        term = dot_t(grad_hidden, weights[c, :, : 2 * slice_])
        if c == 0:
            sum_b[...] = branch
            sum_t[...] = term
        else:
            sum_b[...] += branch
            sum_t[...] += term

    for c in range(min(depth, parts)):
        start_columns(c)
    pair_x[pl.ds(0, tokens)] = normed_ref[...]
    pair_g[pl.ds(0, tokens)] = grad_here_ref[...]
    for c in range(parts + 2):
        if c < parts:
            for k in range(1, columns):
                column_copy(c, k).wait_recv()
            relay(c, lambda copy: copy.start())
            weights[c, pl.ds(pl.multiple_of(me * rows, rows), rows)] = arrived[c][owner_mine]
            stage[c] = arrived[c][owner_other]
            first(c)
            if c + depth < parts:
                start_columns(c + depth)
            second(c)
        if 1 <= c <= parts:
            third(c - 1)
        if c >= 2:
            last(c - 2)
            if c == 2:
                for copy in token_copies():
                    copy.wait()
            work(c - 2)

    back_b[...] = sum_b[pl.ds(tokens, tokens)].astype(jnp.bfloat16)
    back_t[...] = sum_t[pl.ds(tokens, tokens)].astype(jnp.bfloat16)
    backs = [to_sibling(2, back_b, branch_there), to_sibling(3, back_t, term_there)]
    for copy in backs:
        copy.start()
    branch_here[...] = sum_b[pl.ds(0, tokens)].astype(jnp.bfloat16)
    term_here[...] = sum_t[pl.ds(0, tokens)].astype(jnp.bfloat16)
    for c in range(parts):
        for k in range(1, columns):

            @pl.when(sends(k))
            def _():
                column_copy(c, k).wait_send()

        relay(c, lambda copy: copy.wait_send())
        for copy in spreads(c):
            copy.wait_send()
    for copy in backs:
        copy.wait()


def experts(ranks, relays, number, need_lists, gate_up_weight, down_weight, normed, grad_here, grad_there):
    columns = need_lists.shape[0]
    held, rows, width = down_weight.shape
    tokens, model = normed.shape
    slice_ = 128
    parts = width // slice_
    vmem = pl.BlockSpec(memory_space=pltpu.VMEM)
    any_ = pl.BlockSpec(memory_space=pl.ANY)
    sent = 7 if ranks == 8 else ranks - 1
    bf16, f32 = jnp.bfloat16, jnp.float32
    return pl.pallas_call(
        functools.partial(block_kernel, columns, ranks, relays),
        out_shape=[jax.ShapeDtypeStruct((tokens, model), bf16)] * 4,
        in_specs=[pl.BlockSpec(memory_space=pltpu.SMEM), any_, any_, vmem, vmem, vmem],
        out_specs=[vmem] * 4,
        scratch_shapes=[pltpu.VMEM((held, rows, 3 * slice_), bf16) for _ in range(parts)]
        + [pltpu.VMEM((columns, rows, 3 * slice_), bf16) for _ in range(parts)]
        + [
            pltpu.VMEM((parts, columns - 1, rows, 3 * slice_), bf16),
            pltpu.VMEM((parts, rows, 3 * slice_), bf16),
            pltpu.VMEM((parts, ranks * rows, 3 * slice_), bf16),
            pltpu.VMEM((2 * tokens, model), bf16),
            pltpu.VMEM((2 * tokens, model), bf16),
            pltpu.VMEM((2 * tokens, model), f32),
            pltpu.VMEM((2 * tokens, model), f32),
            pltpu.VMEM((tokens, model), bf16),
            pltpu.VMEM((tokens, model), bf16),
            pltpu.SemaphoreType.DMA((parts, 3)),
            pltpu.SemaphoreType.DMA((columns, parts)),
            pltpu.SemaphoreType.DMA((columns - 1, parts)),
            pltpu.SemaphoreType.DMA((sent, parts)),
            pltpu.SemaphoreType.DMA((sent, parts)),
            pltpu.SemaphoreType.DMA((4,)),
            pltpu.SemaphoreType.DMA((4,)),
        ],
        compiler_params=pltpu.CompilerParams(
            collective_id=number, has_side_effects=True, vmem_limit_bytes=56 * 1024 * 1024
        ),
    )(need_lists, gate_up_weight, down_weight, normed, grad_here, grad_there)


def fits(need_lists, held, relays):
    owner_of = need_lists // held
    good = jnp.bool_(True)
    for owner, via, end in relays:
        near = jnp.max(jnp.where(owner_of[via] == owner, need_lists[via], -1))
        far = jnp.max(jnp.where(owner_of[end] == owner, need_lists[end], -1))
        good = good & ((near < 0) | (far < 0) | (near == far))
    return good


def body(
    residual,
    grad_stream,
    expert_gain,
    router_weight,
    gate_up_weight,
    down_weight,
    need_lists,
    routes,
):
    column = lax.axis_index("expert")
    ranks = lax.axis_size("dp")
    parity = lax.axis_index("dp") % 2
    listed = lax.dynamic_index_in_dim(need_lists, column, 0, keepdims=False)
    stream_in = residual.astype(jnp.float32)
    factor_in = norm_factor(stream_in)
    normed = (stream_in * factor_in * expert_gain).astype(jnp.bfloat16)
    router_cols = jnp.take(router_weight, listed, axis=1)
    logits = jnp.dot(normed, router_cols, preferred_element_type=jnp.float32)
    gates = jax.nn.sigmoid(logits - logits[:, ::-1])
    select = (routes == jnp.arange(2, dtype=jnp.int32)[None, :]).astype(jnp.float32)
    mix = gates * select
    mix_here = lax.dynamic_index_in_dim(mix, parity, 1, keepdims=False)
    mix_there = lax.dynamic_index_in_dim(mix, 1 - parity, 1, keepdims=False)
    grad_out = grad_stream.astype(jnp.float32)
    grad_here = (mix_here[:, None] * grad_out).astype(jnp.bfloat16)
    grad_there = (mix_there[:, None] * grad_out).astype(jnp.bfloat16)
    plans = [()]
    if need_lists.shape[0] == 4:
        plans = [((1, 2, 3), (2, 1, 0)), ((0, 2, 3), (2, 1, 0)), ()]
    held = gate_up_weight.shape[0]
    good = [fits(need_lists, held, plan) for plan in plans]
    choice = jnp.int32(len(plans) - 1)
    for i in reversed(range(len(plans) - 1)):
        choice = jnp.where(good[i], i, choice)
    branch_here, branch_there, term_here, term_there = lax.switch(
        choice,
        [functools.partial(experts, ranks, plan, i) for i, plan in enumerate(plans)],
        need_lists,
        gate_up_weight,
        down_weight,
        normed,
        grad_here,
        grad_there,
    )
    branch_here = branch_here.astype(jnp.float32)
    branch_there = branch_there.astype(jnp.float32)
    stream = (
        stream_in + mix_here[:, None] * branch_here + mix_there[:, None] * branch_there
    ).astype(jnp.bfloat16)
    mix_grad_here = jnp.sum(branch_here * grad_out, axis=-1)
    mix_grad_there = jnp.sum(branch_there * grad_out, axis=-1)
    grad_mix = jnp.where(
        parity == 0,
        jnp.stack([mix_grad_here, mix_grad_there], axis=1),
        jnp.stack([mix_grad_there, mix_grad_here], axis=1),
    )
    grad_gates = grad_mix * select
    grad_logits = (
        gates * (grad_gates - jnp.sum(gates * grad_gates, axis=-1, keepdims=True))
    ).astype(jnp.bfloat16)
    grad_normed = term_here.astype(jnp.float32) + term_there.astype(jnp.float32)
    grad_normed = grad_normed + jnp.einsum(
        "tn,dn->td", grad_logits, router_cols, preferred_element_type=jnp.float32
    )
    grad_residual = (
        grad_out + norm_backward(stream_in, factor_in, expert_gain, grad_normed)
    ).astype(jnp.bfloat16)
    return (stream, grad_residual)


def solution(mesh):
    return jax.shard_map(
        body,
        mesh=mesh,
        in_specs=(
            P(("dp", "expert"), None),
            P(("dp", "expert"), None),
            P(),
            P(),
            P("expert", "dp", None),
            P("expert", "dp", None),
            P(),
            P(("dp", "expert"), None),
        ),
        out_specs=(P(("dp", "expert"), None), P(("dp", "expert"), None)),
        check_vma=False,
    )
```

```python
import functools

import jax
import jax.numpy as jnp
from jax import lax
from jax.experimental import pallas as pl
from jax.experimental.pallas import tpu as pltpu
from jax.sharding import PartitionSpec as P

eps = 1e-05
MESH = pl.DeviceIdType.MESH


def norm_factor(values):
    return lax.rsqrt(jnp.mean(values * values, axis=-1, keepdims=True) + eps)


def norm_backward(values, factor, gain, grad):
    scaled = gain * grad
    return factor * scaled - values * factor**3 * jnp.mean(values * scaled, axis=-1, keepdims=True)


def block_kernel(
    columns,
    ranks,
    relays,
    need_ref,
    gate_up_ref,
    down_ref,
    normed_ref,
    grad_here_ref,
    grad_there_ref,
    branch_here,
    branch_there,
    term_here,
    term_there,
    *scratch,
):
    held, rows, _ = down_ref.shape
    width = down_ref.shape[2]
    slice_ = 128
    parts = width // slice_
    tokens = normed_ref.shape[0]
    local = scratch[:parts]
    arrived = scratch[parts : 2 * parts]
    (src, stage, weights, pair_x, pair_g, sum_b, sum_t, back_b, back_t) = scratch[
        2 * parts : 2 * parts + 9
    ]
    ld, zs, zr, ps, pr, ts, tr = scratch[2 * parts + 9 :]
    column = lax.axis_index("expert")
    me = lax.axis_index("dp")
    core = lax.rem(me, 2)
    sibling = me + 1 - 2 * core
    square = ranks == 8
    depth = 2

    def loads(c):
        return [
            pltpu.make_async_copy(
                ref.at[:, :, pl.ds(start, slice_)],
                local[c].at[:, :, pl.ds(i * slice_, slice_)],
                ld.at[c, i],
            )
            for i, (ref, start) in enumerate(
                (
                    (gate_up_ref, c * slice_),
                    (gate_up_ref, width + c * slice_),
                    (down_ref, c * slice_),
                )
            )
        ]

    for c in range(parts):
        for copy in loads(c):
            copy.start()

    if square:
        beside = me + 2 - 4 * lax.rem(me // 2, 2)
        across = me + 4 - 8 * (me // 4)
        peers = [sibling, beside, across]
    else:
        peers = [lax.rem(me + k, ranks) for k in range(1, ranks)]
    barrier = pltpu.get_barrier_semaphore()
    for k in range(1, columns):
        pl.semaphore_signal(
            barrier, inc=1, device_id=(me, lax.rem(column + k, columns)), device_id_type=MESH
        )
    for peer in peers:
        pl.semaphore_signal(barrier, inc=1, device_id=(peer, column), device_id_type=MESH)
    pl.semaphore_wait(barrier, columns - 1 + len(peers))

    def to_sibling(i, source, target):
        return pltpu.make_async_remote_copy(
            src_ref=source,
            dst_ref=target,
            send_sem=ts.at[i],
            recv_sem=tr.at[i],
            device_id=(sibling, column),
            device_id_type=MESH,
        )

    def token_copies():
        return [
            to_sibling(0, normed_ref, pair_x.at[pl.ds(tokens, tokens)]),
            to_sibling(1, grad_there_ref, pair_g.at[pl.ds(tokens, tokens)]),
        ]

    for copy in token_copies():
        copy.start()

    def column_copy(c, k):
        return pltpu.make_async_remote_copy(
            src_ref=src.at[c, k - 1],
            dst_ref=arrived[c].at[column],
            send_sem=zs.at[k - 1, c],
            recv_sem=zr.at[k - 1, c],
            device_id=(me, lax.rem(column + k, columns)),
            device_id_type=MESH,
        )

    def pick(to, found):
        for s in range(2):
            expert = need_ref[to, s]
            found = jnp.where(expert // held == column, expert % held, found)
        return found

    picks = []
    for k in range(columns):
        to = lax.rem(column + k, columns)
        found = jnp.int32(0)
        for owner, via, end in relays:
            if (via - owner) % columns == k:
                found = jnp.where(column == owner, pick(end, found), found)
        picks.append(pick(to, found))

    def sends(k):
        yes = column >= 0
        for owner, via, end in relays:
            if (end - owner) % columns == k:
                yes = yes & (column != owner)
        return yes

    def relay_copy(c, i):
        owner, via, end = relays[i]
        return pltpu.make_async_remote_copy(
            src_ref=arrived[c].at[owner],
            dst_ref=arrived[c].at[owner],
            send_sem=zs.at[columns - 1, c],
            recv_sem=zr.at[(end - owner) % columns - 1, c],
            device_id=(me, end),
            device_id_type=MESH,
        )

    def relay(c, act):
        for i, (owner, via, end) in enumerate(relays):

            @pl.when(column == via)
            def _():
                act(relay_copy(c, i))

    owner_mine = need_ref[column, core] // held
    owner_other = need_ref[column, 1 - core] // held

    def start_columns(c):
        for copy in loads(c):
            copy.wait()
        for k in range(1, columns):
            src[c, k - 1] = local[c][picks[k]]

            @pl.when(sends(k))
            def _():
                column_copy(c, k).start()

        arrived[c][column] = local[c][picks[0]]

    def block(c, rank):
        return weights.at[c, pl.ds(pl.multiple_of(rank * rows, rows), rows)]

    def spread(c, i, source, rank, to):
        return pltpu.make_async_remote_copy(
            src_ref=source,
            dst_ref=block(c, rank),
            send_sem=ps.at[i, c],
            recv_sem=pr.at[i, c],
            device_id=(to, column),
            device_id_type=MESH,
        )

    if square:
        beside_rank = beside
        across_other = across + 1 - 2 * core

        def spreads(c):
            mine, other = block(c, me), stage.at[c]
            return [
                spread(c, 0, other, me, sibling),
                spread(c, 1, mine, me, beside),
                spread(c, 2, mine, me, across),
                spread(c, 3, block(c, sibling), sibling, beside),
                spread(c, 4, block(c, sibling), sibling, across),
                spread(c, 5, block(c, beside_rank), beside_rank, across),
                spread(c, 6, block(c, across_other), across_other, beside),
            ]

        def first(c):
            copies = spreads(c)
            for i in (0, 1, 2):
                copies[i].start()

        def second(c):
            copies = spreads(c)
            copies[0].wait_recv()
            copies[3].start()
            copies[4].start()

        def third(c):
            copies = spreads(c)
            copies[1].wait_recv()
            copies[5].start()
            copies[4].wait_recv()
            copies[6].start()

        def last(c):
            copies = spreads(c)
            for i in (2, 3, 5, 6):
                copies[i].wait_recv()
    else:

        def spreads(c):
            return [
                spread(
                    c,
                    k - 1,
                    block(c, me) if k % 2 == 0 else stage.at[c],
                    me,
                    lax.rem(me + k, ranks),
                )
                for k in range(1, ranks)
            ]

        def first(c):
            for copy in spreads(c):
                copy.start()

        def second(c):
            pass

        def third(c):
            pass

        def last(c):
            for copy in spreads(c):
                copy.wait_recv()

    def dot(left, right):
        return jnp.dot(left, right, preferred_element_type=jnp.float32)

    def dot_t(left, right):
        return lax.dot_general(
            left, right, (((1,), (1,)), ((), ())), preferred_element_type=jnp.float32
        )

    def work(c):
        hidden = dot(pair_x[...], weights[c, :, : 2 * slice_])
        grad_act = dot(pair_g[...], weights[c, :, 2 * slice_ :])
        gate_part = hidden[:, :slice_]
        up_part = hidden[:, slice_:]
        sigma = jax.nn.sigmoid(gate_part)
        silu_gate = gate_part * sigma
        act = (silu_gate * up_part).astype(jnp.bfloat16)
        slope = sigma * (1.0 + gate_part * (1.0 - sigma))
        grad_hidden = jnp.concatenate(
            [grad_act * up_part * slope, grad_act * silu_gate], axis=1
        ).astype(jnp.bfloat16)
        branch = dot_t(act, weights[c, :, 2 * slice_ :])
        term = dot_t(grad_hidden, weights[c, :, : 2 * slice_])
        if c == 0:
            sum_b[...] = branch
            sum_t[...] = term
        else:
            sum_b[...] += branch
            sum_t[...] += term

    for c in range(min(depth, parts)):
        start_columns(c)
    pair_x[pl.ds(0, tokens)] = normed_ref[...]
    pair_g[pl.ds(0, tokens)] = grad_here_ref[...]
    for c in range(parts + 2):
        if c < parts:
            for k in range(1, columns):
                column_copy(c, k).wait_recv()
            relay(c, lambda copy: copy.start())
            weights[c, pl.ds(pl.multiple_of(me * rows, rows), rows)] = arrived[c][owner_mine]
            stage[c] = arrived[c][owner_other]
            first(c)
            if c + depth < parts:
                start_columns(c + depth)
            second(c)
        if 1 <= c <= parts:
            third(c - 1)
        if c >= 2:
            last(c - 2)
            if c == 2:
                for copy in token_copies():
                    copy.wait()
            work(c - 2)

    back_b[...] = sum_b[pl.ds(tokens, tokens)].astype(jnp.bfloat16)
    back_t[...] = sum_t[pl.ds(tokens, tokens)].astype(jnp.bfloat16)
    backs = [to_sibling(2, back_b, branch_there), to_sibling(3, back_t, term_there)]
    for copy in backs:
        copy.start()
    branch_here[...] = sum_b[pl.ds(0, tokens)].astype(jnp.bfloat16)
    term_here[...] = sum_t[pl.ds(0, tokens)].astype(jnp.bfloat16)
    for c in range(parts):
        for k in range(1, columns):

            @pl.when(sends(k))
            def _():
                column_copy(c, k).wait_send()

        relay(c, lambda copy: copy.wait_send())
        for copy in spreads(c):
            copy.wait_send()
    for copy in backs:
        copy.wait()


def experts(ranks, relays, number, need_lists, gate_up_weight, down_weight, normed, grad_here, grad_there):
    columns = need_lists.shape[0]
    held, rows, width = down_weight.shape
    tokens, model = normed.shape
    slice_ = 128
    parts = width // slice_
    vmem = pl.BlockSpec(memory_space=pltpu.VMEM)
    any_ = pl.BlockSpec(memory_space=pltpu.HBM)
    sent = 7 if ranks == 8 else ranks - 1
    bf16, f32 = jnp.bfloat16, jnp.float32
    return pl.pallas_call(
        functools.partial(block_kernel, columns, ranks, relays),
        out_shape=[jax.ShapeDtypeStruct((tokens, model), bf16)] * 4,
        in_specs=[pl.BlockSpec(memory_space=pltpu.SMEM), any_, any_, vmem, vmem, vmem],
        out_specs=[vmem] * 4,
        scratch_shapes=[pltpu.VMEM((held, rows, 3 * slice_), bf16) for _ in range(parts)]
        + [pltpu.VMEM((columns, rows, 3 * slice_), bf16) for _ in range(parts)]
        + [
            pltpu.VMEM((parts, columns - 1, rows, 3 * slice_), bf16),
            pltpu.VMEM((parts, rows, 3 * slice_), bf16),
            pltpu.VMEM((parts, ranks * rows, 3 * slice_), bf16),
            pltpu.VMEM((2 * tokens, model), bf16),
            pltpu.VMEM((2 * tokens, model), bf16),
            pltpu.VMEM((2 * tokens, model), f32),
            pltpu.VMEM((2 * tokens, model), f32),
            pltpu.VMEM((tokens, model), bf16),
            pltpu.VMEM((tokens, model), bf16),
            pltpu.SemaphoreType.DMA((parts, 3)),
            pltpu.SemaphoreType.DMA((columns, parts)),
            pltpu.SemaphoreType.DMA((columns - 1, parts)),
            pltpu.SemaphoreType.DMA((sent, parts)),
            pltpu.SemaphoreType.DMA((sent, parts)),
            pltpu.SemaphoreType.DMA((4,)),
            pltpu.SemaphoreType.DMA((4,)),
        ],
        compiler_params=pltpu.CompilerParams(
            collective_id=number, has_side_effects=True, vmem_limit_bytes=56 * 1024 * 1024
        ),
    )(need_lists, gate_up_weight, down_weight, normed, grad_here, grad_there)


def fits(need_lists, held, relays):
    owner_of = need_lists // held
    good = jnp.bool_(True)
    for owner, via, end in relays:
        near = jnp.max(jnp.where(owner_of[via] == owner, need_lists[via], -1))
        far = jnp.max(jnp.where(owner_of[end] == owner, need_lists[end], -1))
        good = good & ((near < 0) | (far < 0) | (near == far))
    return good


def body(
    residual,
    grad_stream,
    expert_gain,
    router_weight,
    gate_up_weight,
    down_weight,
    need_lists,
    routes,
):
    column = lax.axis_index("expert")
    ranks = lax.axis_size("dp")
    parity = lax.axis_index("dp") % 2
    listed = lax.dynamic_index_in_dim(need_lists, column, 0, keepdims=False)
    stream_in = residual.astype(jnp.float32)
    factor_in = norm_factor(stream_in)
    normed = (stream_in * factor_in * expert_gain).astype(jnp.bfloat16)
    router_cols = jnp.take(router_weight, listed, axis=1)
    logits = jnp.dot(normed, router_cols, preferred_element_type=jnp.float32)
    gates = jax.nn.sigmoid(logits - logits[:, ::-1])
    select = (routes == jnp.arange(2, dtype=jnp.int32)[None, :]).astype(jnp.float32)
    mix = gates * select
    mix_here = lax.dynamic_index_in_dim(mix, parity, 1, keepdims=False)
    mix_there = lax.dynamic_index_in_dim(mix, 1 - parity, 1, keepdims=False)
    grad_out = grad_stream.astype(jnp.float32)
    grad_here = (mix_here[:, None] * grad_out).astype(jnp.bfloat16)
    grad_there = (mix_there[:, None] * grad_out).astype(jnp.bfloat16)
    plans = [()]
    if need_lists.shape[0] == 4:
        plans = [((1, 2, 3), (2, 1, 0)), ()]
    held = gate_up_weight.shape[0]
    good = [fits(need_lists, held, plan) for plan in plans]
    choice = jnp.int32(len(plans) - 1)
    for i in reversed(range(len(plans) - 1)):
        choice = jnp.where(good[i], i, choice)
    branch_here, branch_there, term_here, term_there = lax.switch(
        choice,
        [functools.partial(experts, ranks, plan, i) for i, plan in enumerate(plans)],
        need_lists,
        gate_up_weight,
        down_weight,
        normed,
        grad_here,
        grad_there,
    )
    branch_here = branch_here.astype(jnp.float32)
    branch_there = branch_there.astype(jnp.float32)
    stream = (
        stream_in + mix_here[:, None] * branch_here + mix_there[:, None] * branch_there
    ).astype(jnp.bfloat16)
    mix_grad_here = jnp.sum(branch_here * grad_out, axis=-1)
    mix_grad_there = jnp.sum(branch_there * grad_out, axis=-1)
    grad_mix = jnp.where(
        parity == 0,
        jnp.stack([mix_grad_here, mix_grad_there], axis=1),
        jnp.stack([mix_grad_there, mix_grad_here], axis=1),
    )
    grad_gates = grad_mix * select
    grad_logits = (
        gates * (grad_gates - jnp.sum(gates * grad_gates, axis=-1, keepdims=True))
    ).astype(jnp.bfloat16)
    grad_normed = term_here.astype(jnp.float32) + term_there.astype(jnp.float32)
    grad_normed = grad_normed + jnp.einsum(
        "tn,dn->td", grad_logits, router_cols, preferred_element_type=jnp.float32
    )
    grad_residual = (
        grad_out + norm_backward(stream_in, factor_in, expert_gain, grad_normed)
    ).astype(jnp.bfloat16)
    return (stream, grad_residual)


def solution(mesh):
    return jax.shard_map(
        body,
        mesh=mesh,
        in_specs=(
            P(("dp", "expert"), None),
            P(("dp", "expert"), None),
            P(),
            P(),
            P("expert", "dp", None),
            P("expert", "dp", None),
            P(),
            P(("dp", "expert"), None),
        ),
        out_specs=(P(("dp", "expert"), None), P(("dp", "expert"), None)),
        check_vma=False,
    )
```
